128 devices in a mesh: dom: 128 (over z, y, x, core).
Axes of the slice: x: 4, y: 4, z: 4, core: 2. Of those that a mesh axis runs over, the one named last changes fastest.
Arguments:
- control: float32 [1024, 2048], P('dom'), may hold values from -6 to 6
- reads: int32 [128, 4], replicated, may hold values from 0 to 1023, as said below
- neighbours: int32 [128, 4], replicated, may hold values from 0 to 127, as said below
- halo_cells: int32 [128, 4, 512], P('dom'), may hold values from 0 to 65535
- wet_mask: int32 [8388608], P('dom'), may hold values 0 or 1
- depth: float32 [8388608], P('dom'), may hold values from 1 to 2
- sensitivity: float32 [8388608], P('dom'), may hold values from -3.25 to 3.25
- obs_weight: float32 [8388608], P('dom'), may hold values from 0.2 to 2
- basis_rows: float32 [128, 4, 32, 128], P('dom'), may hold values from -1 to 1
- basis_cols: float32 [128, 4, 64, 512], P('dom'), may hold values from -0.75 to 0.75
Outputs:
- hessian_vec: float32 [1024, 2048], P('dom')
- weighted_obs: float32 [8388608], P('dom')
The draws below stay inside these ranges and needn't reach their ends.
Inputs may be any that keep to these rules, and one draw needn't show every extreme that they name: `reads`: block b is owned by partition b // 8. Each row lists distinct blocks, in no particular order and from owners anywhere on the axis; at most 2 of a row belong to one owner, and every row has exactly 2 from one owner. `neighbours`: each row lists 4 distinct partitions other than its own; q is in row p exactly when p is in row q. `halo_cells`: local cell indices of the partition.
All inputs are finite; a program needn't handle non-finite values. No bound on the sum of `wet_mask` on one device may be relied on, other than what follows from the above.
Results may differ from the reference program's by a relative error of at most 0.000071.
Values sent between devices are 32-bit elements; how exact they have to be, the bound alone decides.
A program may use at most 64 MiB of HBM per device.

```python
import math
import jax
import jax.numpy as jnp
from jax import lax

PR = 128
PC = 512
STEPS = 12
KX = 32
KY = 64
OWN = 8
READS = 4
NB = 4
HC = 512
CELLS = 8388608
KC = 2048
BLOCKS = 1024
N_DOM = 128


def draw_reads(key, part):
    n = N_DOM
    rows = jnp.arange(n, dtype=jnp.int32)
    k_first = jax.random.fold_in(key, 11)
    k_second = jax.random.fold_in(key, 12)
    k_third = jax.random.fold_in(key, 13)
    k_fourth = jax.random.fold_in(key, 14)
    k_base = jax.random.fold_in(key, 15)
    k_deltb = jax.random.fold_in(key, 16)
    k_deltc = jax.random.fold_in(key, 17)
    k_forced = jax.random.fold_in(key, 18)
    k_order = jax.random.fold_in(key, 19)
    base_off = jax.random.randint(k_base, (n,), 0, n)
    delta_b = jax.random.randint(k_deltb, (n,), 1, n)
    delta_c = jax.random.randint(k_deltc, (n,), 1, n)
    forced = jax.random.permutation(k_forced, n)
    is_half = rows == forced[0]
    is_next = rows == forced[1]
    is_prev = rows == forced[2]
    any_forced = is_half | is_next | is_prev
    base_off = jnp.where(any_forced, 0, base_off)
    target = jnp.where(is_half, n // 2, jnp.where(is_next, 1, n - 1))
    delta_b = jnp.where(any_forced, target, delta_b)
    owner_a = (rows + base_off) % n
    owner_b = (owner_a + delta_b) % n
    owner_c = (owner_a + delta_c) % n
    first = jax.random.randint(k_first, (n,), 0, OWN)
    second = (first + jax.random.randint(k_second, (n,), 1, OWN)) % OWN
    third = jax.random.randint(k_third, (n,), 0, OWN)
    fourth = (third + jax.random.randint(k_fourth, (n,), 1, OWN)) % OWN
    cols = jnp.stack([owner_a * OWN + first, owner_a * OWN + second, owner_b * OWN + third, owner_c * OWN + fourth], axis=1)
    scores = jax.random.randint(k_order, (n, 4), 0, 1000) * 4 + jnp.arange(4, dtype=jnp.int32)[None, :]
    order = jnp.argsort(scores, axis=1)
    return jnp.take_along_axis(cols, order, axis=1).astype(jnp.int32)


def draw_neighbours(key, part):
    n = N_DOM
    kstep = jax.random.fold_in(key, 21)
    korder = jax.random.fold_in(key, 22)
    klabel = jax.random.fold_in(key, 23)
    stride = jax.random.randint(kstep, (), 2, n // 2)
    posit = jnp.arange(n, dtype=jnp.int32)
    label = jax.random.permutation(klabel, n).astype(jnp.int32)
    target_one = (label[0] + n // 2) % n
    where_one = jnp.sum(jnp.where(label == target_one, posit, 0)).astype(jnp.int32)
    label = label.at[where_one].set(label[1]).at[1].set(target_one)
    target_two = (target_one + 1) % n
    where_two = jnp.sum(jnp.where(label == target_two, posit, 0)).astype(jnp.int32)
    label = label.at[where_two].set(label[2]).at[2].set(target_two)
    inverse = jnp.zeros((n,), jnp.int32).at[label].set(posit)
    place = inverse
    base = jnp.stack([label[(place + 1) % n], label[(place - 1 + n) % n], label[(place + stride) % n], label[(place - stride + n) % n]], axis=1)
    scores = jax.random.randint(korder, (n, 4), 0, 1000) * 4 + jnp.arange(4, dtype=jnp.int32)[None, :]
    order = jnp.argsort(scores, axis=1)
    return jnp.take_along_axis(base, order, axis=1).astype(jnp.int32)


def draw_depth(key, part):
    key = jax.random.fold_in(key, 31)
    values = jax.random.uniform(key, (CELLS,), jnp.float32, 1.0, 2.0)
    return values


def draw_sensitivity(key, part):
    key = jax.random.fold_in(key, 41)
    cell = jnp.arange(CELLS, dtype=jnp.int32) % (PR * PC)
    parity = (cell // PC + cell % PC) % 2
    signs = 1.0 - 2.0 * parity.astype(jnp.float32)
    magnitude = 0.25 + jnp.minimum(jnp.abs(jax.random.normal(key, (CELLS,), jnp.float32)), 3.0)
    return signs * magnitude


def place_ends(array, key, smallest, high):
    dims = array.shape
    index_at = [jax.random.randint(jax.random.fold_in(key, axis), (), 0, dims[axis]) for axis in range(len(dims))]
    array = array.at[tuple(index_at)].set(smallest)
    longest = dims.index(max(dims))
    index_at[longest] = (index_at[longest] + 1) % dims[longest]
    return array.at[tuple(index_at)].set(high)


def block_scale(stream_key, shape, pieces, least, largest):
    loudness, own = 1.0, jax.random.fold_in(stream_key, 6)
    for axis_at, shards_of in pieces:
        draws = jnp.exp(jax.random.uniform(jax.random.fold_in(own, axis_at), (shards_of,), jnp.float32, least / len(pieces), largest / len(pieces)))
        loudness = loudness * jnp.repeat(draws, shape[axis_at] // shards_of).reshape([-1 if axis == axis_at else 1 for axis in range(len(shape))])
    return loudness


def gaussian(rng, extent, spread, limit, cuts=(), held_as=jnp.bfloat16):
    result = spread * jax.random.normal(rng, extent, jnp.float32)
    if cuts:
        result = result * block_scale(rng, extent, cuts, -0.22, 0.18)
    return jnp.clip(result, -limit, limit).astype(held_as)


def setup_inputs(seed: int = 0) -> dict:
    splits = jax.random.split(jax.random.key(seed), 11)
    control = gaussian(splits[0], (BLOCKS, KC), 1.0, 6.0, ((0, 128),), jnp.float32)
    reads = draw_reads(jax.random.fold_in(splits[10], 71), 0)
    neighbours = draw_neighbours(jax.random.fold_in(splits[10], 71), 0)
    halo_cells = place_ends(jax.random.randint(splits[3], (N_DOM, NB, HC), 0, PR * PC), jax.random.fold_in(splits[3], 1), 0, (PR * PC) - 1).astype(jnp.int32)
    wet_mask = place_ends((jax.random.randint(splits[4], (CELLS,), 0, 4) < 3).astype(jnp.int32), jax.random.fold_in(splits[4], 1), 0, 1)
    depth = draw_depth(jax.random.fold_in(splits[10], 71), 0)
    sensitivity = draw_sensitivity(jax.random.fold_in(splits[10], 71), 0)
    obs_weight = jnp.clip(jnp.exp(math.log(2.0) - 2.3025851 * jax.random.uniform(splits[7], (CELLS,), jnp.float32) ** block_scale(splits[7], (CELLS,), ((0, 128),), -0.2, 0.2)), 0.2, 2.0)
    basis_rows = gaussian(splits[8], (N_DOM, READS, KX, PR), KX ** -0.5, 1.0, ((0, 128),), jnp.float32)
    basis_cols = gaussian(splits[9], (N_DOM, READS, KY, PC), KY ** -0.5, 0.75, ((0, 128),), jnp.float32)
    return dict(control=control, reads=reads, neighbours=neighbours, halo_cells=halo_cells, wet_mask=wet_mask, depth=depth, sensitivity=sensitivity, obs_weight=obs_weight, basis_rows=basis_rows, basis_cols=basis_cols)


HIGH = lax.Precision.HIGHEST

def lap_all(field, depth, halo_cells, neighbours, partner):
    ndev = field.shape[0]
    grid = field.reshape(ndev, PR, PC)
    hgrid = depth.reshape(ndev, PR, PC)
    wrow = 0.5 * (hgrid[:, :, :-1] + hgrid[:, :, 1:])
    frow = wrow * (grid[:, :, :-1] - grid[:, :, 1:])
    wcol = 0.5 * (hgrid[:, :-1, :] + hgrid[:, 1:, :])
    fcol = wcol * (grid[:, :-1, :] - grid[:, 1:, :])
    zero = jnp.float32(0.0)
    out = jnp.pad(frow, ((0, 0), (0, 0), (0, 1))) - jnp.pad(frow, ((0, 0), (0, 0), (1, 0)))
    out = out + jnp.pad(fcol, ((0, 0), (0, 1), (0, 0))) - jnp.pad(fcol, ((0, 0), (1, 0), (0, 0)))
    out = out.reshape(ndev, PR * PC)
    other = halo_cells[neighbours, partner]
    nbr_rows = neighbours[:, :, None] * jnp.ones_like(other)
    own_rows = (jnp.arange(ndev, dtype=jnp.int32)[:, None, None] * jnp.ones_like(other)).astype(jnp.int32)
    ghost_val = field[nbr_rows, other]
    ghost_dep = depth[nbr_rows, other]
    edge_w = 0.5 * (depth[own_rows, halo_cells] + ghost_dep)
    out = out.at[own_rows, halo_cells].add(edge_w * (field[own_rows, halo_cells] - ghost_val))
    return out + zero

def reference(control, reads, neighbours, halo_cells, wet_mask, depth, sensitivity, obs_weight, basis_rows, basis_cols):
    ndev = N_DOM
    ids = jnp.arange(ndev, dtype=jnp.int32)
    slots = jnp.arange(NB, dtype=jnp.int32)
    match = (neighbours[neighbours] == ids[:, None, None]).astype(jnp.int32)
    partner = lax.optimization_barrier(jnp.sum(match * slots[None, None, :], axis=-1)).astype(jnp.int32)
    dep = depth.reshape(ndev, PR * PC)
    kw = 0.11 * wet_mask.astype(jnp.float32).reshape(ndev, PR * PC)
    sens = sensitivity.reshape(ndev, PR * PC)
    weight = obs_weight.reshape(ndev, PR * PC)

    def forward(ctl):
        blocks = ctl[reads].reshape(ndev, READS, KX, KY)
        inner = jnp.einsum('nrkl,nrlb->nrkb', blocks, basis_cols, precision=HIGH)
        bathy = jnp.einsum('nrka,nrkb->nab', basis_rows, inner, precision=HIGH).reshape(ndev, PR * PC)
        source = kw * sens * bathy
        elev = jnp.zeros((ndev, PR * PC), jnp.float32)
        for step in range(STEPS):
            elev = elev - kw * lap_all(elev, dep, halo_cells, neighbours, partner) + source
        return elev
    elev, pullback = jax.vjp(forward, control)
    obs = weight * elev
    hess = pullback(obs)[0]
    return (hess, obs.reshape(-1))
```

```python
import jax
import jax.numpy as jnp
from jax import lax
from jax.experimental import pallas as pl
from jax.experimental.pallas import tpu as pltpu
from jax.sharding import PartitionSpec as P

STEPS = 12
KAPPA = 0.11
HIGH = lax.Precision.HIGHEST
MESH = pl.DeviceIdType.MESH
F32 = jnp.float32
BF16 = jnp.bfloat16

NDEV = 128
LOW = 8
HIGHN = 16
ROWS, COLS = 128, 512
NB, READS, OWN = 4, 4, 8
CH = 16


def ring(d):
    return (0, 1, 2, 1)[d]


def hops(m):
    return ring((m >> 1) & 3) + ring((m >> 3) & 3) + ring((m >> 5) & 3)


FAR_FIRST = sorted(range(1, NDEV), key=lambda m: -hops(m))


def flip(value, mask, bits):
    out = value
    for i in range(bits):
        if (mask >> i) & 1:
            bit = lax.rem(lax.div(value, 1 << i), 2)
            out = out + (1 - 2 * bit) * (1 << i)
    return out


def differ(a, b, bits):
    out = 0
    for i in range(bits):
        d = lax.rem(lax.div(a, 1 << i), 2) - lax.rem(lax.div(b, 1 << i), 2)
        out = out + d * d * (1 << i)
    return out


def dot(a, b, precision=None):
    return jnp.dot(a, b, precision=precision, preferred_element_type=F32)


def halves(v):
    high = v.astype(BF16).astype(F32)
    return high, v - high


def kernel(
    tab, control, cells, wet, depth, sens, obs, brows, bcols,
    hess, wobs,
    kw, wr, wd, dia, src, bgr, ends, pick, pickt, spread, uone, uonet,
    row16, col16, uhi16, ulo16, mins, ew, kwj, xg, gx, fx, pg, sbuf, rbuf, lin,
    ph1, sb2, rb2, gr, sp, rp, wt, uall, inner, acc, kid,
    ssem, rsem, s1, r1, s2, r2, s3, r3, s4, r4,
):
    me = lax.axis_index("dom")
    my_low = lax.rem(me, LOW)
    my_high = lax.div(me, LOW)
    low_of = [flip(my_low, m, 3) for m in range(LOW)]
    high_of = [flip(my_high, m, 4) * LOW for m in range(HIGHN)]

    def peer(m):
        return high_of[m >> 3] + low_of[m & 7]

    barrier = pltpu.get_barrier_semaphore()
    for m in FAR_FIRST:
        pl.semaphore_signal(barrier, inc=1, device_id=(peer(m),), device_id_type=MESH)

    for i in range(CH):
        ph1[0:OWN, i, :] = control[:, i * 128:(i + 1) * 128]
    for k in range(NB):
        for c in range(4):
            part = cells[0, k:k + 1, c * 128:(c + 1) * 128]
            row16[4 * k + c:4 * k + c + 1, :] = lax.div(part, COLS)
            col16[4 * k + c:4 * k + c + 1, :] = lax.rem(part, COLS)
    up = lax.broadcasted_iota(jnp.int32, (ROWS, 128), 0)
    across = lax.broadcasted_iota(jnp.int32, (128, 128), 1)
    tall = lax.broadcasted_iota(jnp.int32, (COLS, 128), 0)
    for j in range(CH):
        pick[:, j * 128:(j + 1) * 128] = jnp.where(
            tall == col16[j:j + 1, :], 1.0, 0.0
        ).astype(BF16)
    nbr = [tab[READS + k, me] for k in range(NB)]
    at = [differ(nbr[k], me, 7) for k in range(NB)]
    lin[0] = jnp.zeros((4, 128), F32)

    def find_slot(q, carry):
        last = jnp.where(nbr[2] == q, 2, jnp.where(nbr[3] == q, 3, 0))
        kid[q] = jnp.where(nbr[1] == q, 1, last)
        return carry

    lax.fori_loop(0, NDEV, find_slot, 0)

    def take(field, out):
        high, low = halves(field)
        both = jnp.concatenate([high.astype(BF16), low.astype(BF16)], axis=0)
        for jj in range(CH // 2):
            lifted = dot(both, pick[:, jj * 256:(jj + 1) * 256])
            lifted = lifted[:ROWS] + lifted[ROWS:]
            for h in range(2):
                j = 2 * jj + h
                mine = jnp.where(
                    up == row16[j:j + 1, :], lifted[:, h * 128:(h + 1) * 128], 0.0
                )
                out[j:j + 1, :] = jnp.sum(mine, axis=0, keepdims=True)

    def put(values):
        high, low = halves(values)
        for j in range(CH):
            at_row = up == row16[j:j + 1, :]
            spread[0:ROWS, j * 128:(j + 1) * 128] = jnp.where(
                at_row, high[j:j + 1, :], 0.0
            ).astype(BF16)
            spread[ROWS:2 * ROWS, j * 128:(j + 1) * 128] = jnp.where(
                at_row, low[j:j + 1, :], 0.0
            ).astype(BF16)
        placed = dot(spread[...], pickt[...])
        return placed[:ROWS] + placed[ROWS:]

    few = lax.broadcasted_iota(jnp.int32, (CH, 128), 0)

    def same_cell(values):
        high, low = halves(values)
        mine = [few == uhi16[j:j + 1, :] for j in range(CH)]
        spread_h = [jnp.where(mine[j], high[j:j + 1, :], 0.0) for j in range(CH)]
        spread_l = [jnp.where(mine[j], low[j:j + 1, :], 0.0) for j in range(CH)]
        both = jnp.concatenate(
            [jnp.concatenate(spread_h, axis=1), jnp.concatenate(spread_l, axis=1)], axis=0
        ).astype(BF16)
        table = dot(both, uone[...])
        high, low = halves(table[:CH] + table[CH:])
        lifted = dot(jnp.concatenate([high, low], axis=0).astype(BF16), uonet[...])
        lifted = lifted[:CH] + lifted[CH:]
        rows = [
            jnp.sum(
                jnp.where(mine[j], lifted[:, j * 128:(j + 1) * 128], 0.0),
                axis=0,
                keepdims=True,
            )
            for j in range(CH)
        ]
        return jnp.concatenate(rows, axis=0)

    def send(values, parity):
        for k in range(NB):
            fx[k] = values[4 * k:4 * k + 4, :]
        for m in FAR_FIRST:
            there = peer(m)
            sbuf[m - 1] = fx[kid[there]]
            pltpu.make_async_remote_copy(
                sbuf.at[m - 1], rbuf.at[parity, m - 1], ssem, rsem.at[parity],
                device_id=(there,), device_id_type=MESH,
            ).start()

    def receive(parity):
        whole = pltpu.make_async_remote_copy(
            sbuf, rbuf.at[parity], ssem, rsem.at[parity],
            device_id=(peer(1),), device_id_type=MESH,
        )
        whole.wait_recv()
        lin[1:NDEV] = rbuf[parity]
        for k in range(NB):
            gx[4 * k:4 * k + 4, :] = lin[at[k]]
        whole.wait_send()

    def wait_all(sent, arrived, size, count, send_sem, recv_sem):
        pltpu.make_async_remote_copy(
            sent.at[pl.ds(size, size * count)], arrived.at[pl.ds(size, size * count)],
            send_sem, recv_sem, device_id=(peer(1),), device_id_type=MESH,
        ).wait()

    def patch(v):
        right = wr[...] * (v - pltpu.roll(v, COLS - 1, 1))
        down = wd[...] * (v - pltpu.roll(v, ROWS - 1, 0))
        return right - pltpu.roll(right, 1, 1) + down - pltpu.roll(down, 1, 0)

    def unfold(ref, c):
        return ref[pl.ds(c, ROWS, stride=4), :]

    def grid(ref):
        return jnp.concatenate([unfold(ref, c) for c in range(4)], axis=1)

    h = grid(depth)
    take(h, xg)

    pl.semaphore_wait(barrier, NDEV - 1)

    blk = OWN * CH
    first = [
        pltpu.make_async_remote_copy(
            ph1.at[pl.ds(0, OWN)], ph1.at[pl.ds(m * OWN, OWN)], s1, r1,
            device_id=(peer(m),), device_id_type=MESH,
        )
        for m in range(1, LOW)
    ]
    for copy in first:
        copy.start()
    send(xg[...], 1)

    last_col = lax.broadcasted_iota(jnp.int32, (ROWS, COLS), 1) == COLS - 1
    last_row = lax.broadcasted_iota(jnp.int32, (ROWS, COLS), 0) == ROWS - 1
    wr[...] = jnp.where(last_col, 0.0, 0.5 * (h + pltpu.roll(h, COLS - 1, 1)))
    wd[...] = jnp.where(last_row, 0.0, 0.5 * (h + pltpu.roll(h, ROWS - 1, 0)))
    mask = grid(wet).astype(F32)
    kw[...] = KAPPA * mask
    take(mask, kwj)
    kwj[...] = KAPPA * kwj[...]

    mins[...] = jnp.full((CH * 8, 128), 4096.0, F32)

    def earliest(i, carry):
        mine = row16[pl.ds(i, 1), :] * COLS + col16[pl.ds(i, 1), :]
        column = jnp.transpose(jnp.broadcast_to(mine.astype(F32), (128, 128)))
        number = (up + i * 128).astype(F32)
        for j in range(CH):
            other = (row16[j:j + 1, :] * COLS + col16[j:j + 1, :]).astype(F32)
            found = jnp.where(column == other, number, 4096.0)
            found = jnp.min(found.reshape(16, 8, 128), axis=0)
            mins[8 * j:8 * j + 8, :] = jnp.minimum(mins[8 * j:8 * j + 8, :], found)
        return carry

    lax.fori_loop(0, CH, earliest, 0)
    for j in range(CH):
        u = jnp.min(mins[8 * j:8 * j + 8, :], axis=0, keepdims=True).astype(jnp.int32)
        uhi16[j:j + 1, :] = lax.div(u, 128)
        ulo16[j:j + 1, :] = lax.rem(u, 128)
    for j in range(CH):
        ulo = ulo16[j:j + 1, :]
        uonet[:, j * 128:(j + 1) * 128] = jnp.where(up == ulo, 1.0, 0.0).astype(BF16)
        column = jnp.transpose(jnp.broadcast_to(ulo.astype(F32), (128, 128)))
        uone[j * 128:(j + 1) * 128, :] = jnp.where(
            column == across.astype(F32), 1.0, 0.0
        ).astype(BF16)
        column = jnp.transpose(
            jnp.broadcast_to(col16[j:j + 1, :].astype(F32), (128, 128))
        )
        for c in range(4):
            pickt[j * 128:(j + 1) * 128, c * 128:(c + 1) * 128] = jnp.where(
                column == (across + c * 128).astype(F32), 1.0, 0.0
            ).astype(BF16)

    wait_all(ph1, ph1, OWN, LOW - 1, s1, r1)
    part = READS * CH
    for j in range(HIGHN):
        reader = high_of[j] + my_low
        for k in range(READS):
            b = tab[k, reader]
            owner = lax.div(b, OWN)
            index = differ(lax.rem(owner, LOW), my_low, 3) * OWN + lax.rem(b, OWN)
            if j == 0:
                rb2[k] = ph1[index]
            else:
                sb2[j * READS + k] = ph1[index]
        if j:
            pltpu.make_async_remote_copy(
                sb2.at[pl.ds(j * READS, READS)], rb2.at[pl.ds(j * READS, READS)], s2, r2,
                device_id=(reader,), device_id_type=MESH,
            ).start()

    receive(1)
    ew[...] = 0.5 * (xg[...] + gx[...])
    dia[...] = put(ew[...])
    for r in range(READS):
        for p in range(2):
            uall[p * 64 + r * CH:p * 64 + (r + 1) * CH, :] = brows[
                0, r, pl.ds(p, CH, stride=2), :
            ]
    wait_all(sb2, rb2, READS, HIGHN - 1, s2, r2)

    zero = jnp.zeros((64, COLS), F32)
    for k in range(READS):
        owner = lax.div(tab[k, me], OWN)
        row = differ(lax.div(owner, LOW), my_high, 4)
        block = rb2[row * READS + k]
        uy = bcols[0, k]
        inner[k * CH:(k + 1) * CH, :] = dot(block, jnp.concatenate([uy, zero], 0), HIGH)
        inner[64 + k * CH:64 + (k + 1) * CH, :] = dot(
            block, jnp.concatenate([zero, uy], 0), HIGH
        )
    bathy = dot(jnp.transpose(uall[...]), inner[...], HIGH)
    src[...] = kw[...] * grid(sens) * bathy

    def run(phase, carry):
        s = src[...]
        bgr[...] = s
        take(s, pg)
        gx[...] = jnp.zeros((CH, 128), F32)
        fx16 = pg

        def step(n, c):
            parity = lax.rem(phase * (STEPS - 1) + n, 2)
            send(fx16[...], parity)
            k = kw[...]
            e = bgr[...] + k * put(gx[...])
            new = e - k * (patch(e) + dia[...] * e) + src[...]
            bgr[...] = new
            take(new, pg)
            receive(parity)
            x = ew[...] * gx[...]
            gx[...] = x
            pg[...] = pg[...] + kwj[...] * same_cell(x)
            return c

        lax.fori_loop(0, STEPS - 1, step, 0)
        e = bgr[...] + kw[...] * put(gx[...])
        ends[phase] = e
        src[...] = kw[...] * (grid(obs) * e)
        return carry

    lax.fori_loop(0, 2, run, 0)
    seen = grid(obs) * ends[0]
    for c in range(4):
        wobs[pl.ds(c, ROWS, stride=4), :] = seen[:, c * 128:(c + 1) * 128]

    grad = grid(sens) * ends[1]
    side = dot(uall[...], grad, HIGH)
    for r in range(READS):
        uy = bcols[0, r]
        even = lax.dot_general(
            side[r * CH:(r + 1) * CH], jnp.concatenate([uy, zero], 0),
            (((1,), (1,)), ((), ())), precision=HIGH, preferred_element_type=F32,
        )
        odd = lax.dot_general(
            side[64 + r * CH:64 + (r + 1) * CH], jnp.concatenate([zero, uy], 0),
            (((1,), (1,)), ((), ())), precision=HIGH, preferred_element_type=F32,
        )
        gr[r * CH:(r + 1) * CH, :] = even + odd

    third = [
        pltpu.make_async_remote_copy(
            gr.at[pl.ds(0, part)], gr.at[pl.ds(j * part, part)], s3, r3,
            device_id=(high_of[j] + my_low,), device_id_type=MESH,
        )
        for j in range(1, HIGHN)
    ]
    for copy in third:
        copy.start()
    lane = lax.broadcasted_iota(jnp.int32, (1, 128), 1)
    wt[...] = jnp.zeros((128, 128), F32)
    for j in range(HIGHN):
        for k in range(READS):
            b = tab[k, high_of[j] + my_low]
            owner = lax.div(b, OWN)
            index = differ(lax.rem(owner, LOW), my_low, 3) * OWN + lax.rem(b, OWN)
            index = jnp.where(lax.div(owner, LOW) == my_high, index, -1)
            s = j * READS + k
            wt[s:s + 1, :] = jnp.where(lane == index, 1.0, 0.0)
    gather = jnp.transpose(wt[...])[:64, :64]
    wait_all(gr, gr, part, HIGHN - 1, s3, r3)
    for i in range(CH):
        sp[pl.ds(i, 64, stride=CH), :] = dot(gather, gr[pl.ds(i, 64, stride=CH), :], HIGH)
    fourth = [
        pltpu.make_async_remote_copy(
            sp.at[pl.ds(m * blk, blk)], rp.at[pl.ds(m * blk, blk)], s4, r4,
            device_id=(peer(m),), device_id_type=MESH,
        )
        for m in range(1, LOW)
    ]
    for copy in fourth:
        copy.start()
    wait_all(sp, rp, blk, LOW - 1, s4, r4)
    total = sp[0:blk, :]
    for m in range(1, LOW):
        total = total + rp[m * blk:(m + 1) * blk, :]
    acc[...] = total
    for i in range(CH):
        hess[:, i * 128:(i + 1) * 128] = acc[pl.ds(i, OWN, stride=CH), :]


def on_device(
    control, reads, neighbours, halo_cells, wet_mask, depth, sensitivity, obs_weight,
    basis_rows, basis_cols,
):
    table = jnp.concatenate([reads, neighbours], axis=1).T
    flat = (ROWS * COLS // 128, 128)
    field = pltpu.VMEM((ROWS, COLS), F32)
    few = pltpu.VMEM((CH, 128), F32)
    few_int = pltpu.VMEM((CH, 128), jnp.int32)
    edges = CH * 128
    blocks = pltpu.VMEM((LOW * OWN * CH, 128), F32)
    apart = pltpu.VMEM((LOW * OWN, CH, 128), F32)
    dma = pltpu.SemaphoreType.DMA
    vmem = pl.BlockSpec(memory_space=pltpu.VMEM)
    hess, wobs = pl.pallas_call(
        kernel,
        name="hessian_product",
        out_shape=(
            jax.ShapeDtypeStruct(control.shape, F32),
            jax.ShapeDtypeStruct(flat, F32),
        ),
        in_specs=[pl.BlockSpec(memory_space=pltpu.SMEM)] + [vmem] * 8,
        out_specs=(vmem, vmem),
        scratch_shapes=[
            field, field, field, field, field, field,
            pltpu.VMEM((2, ROWS, COLS), F32),
            pltpu.VMEM((COLS, edges), BF16),
            pltpu.VMEM((edges, COLS), BF16),
            pltpu.VMEM((2 * ROWS, edges), BF16),
            pltpu.VMEM((edges, 128), BF16),
            pltpu.VMEM((128, edges), BF16),
            few_int, few_int, few_int, few_int,
            pltpu.VMEM((CH * 8, 128), F32),
            few, few, few, few,
            pltpu.VMEM((NB, 4, 128), F32),
            few,
            pltpu.VMEM((NDEV - 1, 4, 128), F32),
            pltpu.VMEM((2, NDEV - 1, 4, 128), F32),
            pltpu.VMEM((NDEV, 4, 128), F32),
            apart, apart, apart, blocks, blocks, blocks,
            pltpu.VMEM((128, 128), F32),
            pltpu.VMEM((128, 128), F32),
            pltpu.VMEM((128, COLS), F32),
            pltpu.VMEM((OWN * CH, 128), F32),
            pltpu.SMEM((NDEV,), jnp.int32),
            dma, dma((2,)), dma, dma, dma, dma, dma, dma, dma, dma,
        ],
        compiler_params=pltpu.CompilerParams(
            collective_id=0, has_side_effects=True, vmem_limit_bytes=48 << 20
        ),
    )(
        table, control, halo_cells, wet_mask.reshape(flat), depth.reshape(flat),
        sensitivity.reshape(flat), obs_weight.reshape(flat), basis_rows, basis_cols,
    )
    return hess, wobs.reshape(-1)


def solution(mesh):
    return jax.shard_map(
        on_device,
        mesh=mesh,
        in_specs=(
            P("dom", None), P(), P(), P("dom", None, None), P("dom"), P("dom"), P("dom"),
            P("dom"), P("dom", None, None, None), P("dom", None, None, None),
        ),
        out_specs=(P("dom", None), P("dom")),
        check_vma=False,
    )
```

```python
import random

import jax
import jax.numpy as jnp
from jax import lax
from jax.experimental import pallas as pl
from jax.experimental.pallas import tpu as pltpu
from jax.sharding import PartitionSpec as P

STEPS = 12
TURN = STEPS - 1
KAPPA = 0.11
HIGH = lax.Precision.HIGHEST
MESH = pl.DeviceIdType.MESH
F32 = jnp.float32
BF16 = jnp.bfloat16

NDEV = 128
LOW = 8
HIGHN = 16
ROWS, COLS = 128, 512
NB, READS, OWN = 4, 4, 8
PIECES = 4
CH = 16
PR = CH // PIECES


def ring(d):
    return (0, 1, 2, 1)[d]


def hops(m):
    return ring((m >> 1) & 3) + ring((m >> 3) & 3) + ring((m >> 5) & 3)


def far_first():
    order = list(range(1, NDEV))
    random.Random(1).shuffle(order)
    return sorted(order, key=lambda m: -hops(m))


FAR_FIRST = far_first()


def flip(value, mask, bits):
    out = value
    for i in range(bits):
        if (mask >> i) & 1:
            bit = lax.rem(lax.div(value, 1 << i), 2)
            out = out + (1 - 2 * bit) * (1 << i)
    return out


def differ(a, b, bits):
    out = 0
    for i in range(bits):
        d = lax.rem(lax.div(a, 1 << i), 2) - lax.rem(lax.div(b, 1 << i), 2)
        out = out + d * d * (1 << i)
    return out


def dot(a, b, precision=None):
    return jnp.dot(a, b, precision=precision, preferred_element_type=F32)


def halves(v):
    high = v.astype(BF16).astype(F32)
    return high, v - high


def kernel(
    reads, nbrs, control_hbm, cells_hbm, wet_hbm, depth_hbm, sens_hbm, obs_hbm,
    brows_hbm, bcols_hbm,
    hess, wobs,
    control, cells, wet, depth, sens, obs, brows, bcols, insem,
    kw, wr, wd, dia, src, bgr, wgt, obj, seen, pick, pickt, spread, uone,
    row16, col16, uhi16, ulo16, mins, ew, kwj, xg, gx, fx, pg, sbuf, rbuf0, rbuf1,
    ph1a, ph1b, ph1c, ph1d, sb2, rb2, gr, sp, rp, wt, uall, acc, kid,
    ssem, rsem, s1, r1, s2, r2, s3, r3, s4, r4,
):
    names = (control, cells, depth, wet, brows, bcols, sens, obs)
    sources = (
        control_hbm, cells_hbm, depth_hbm, wet_hbm, brows_hbm, bcols_hbm, sens_hbm, obs_hbm
    )
    loads = [
        pltpu.make_async_copy(a, b, insem.at[i])
        for i, (a, b) in enumerate(zip(sources, names))
    ]
    for load in loads:
        load.start()
    me = lax.axis_index("dom")
    my_low = lax.rem(me, LOW)
    my_high = lax.div(me, LOW)
    low_of = [flip(my_low, m, 3) for m in range(LOW)]
    high_of = [flip(my_high, m, 4) * LOW for m in range(HIGHN)]

    def peer(m):
        return high_of[m >> 3] + low_of[m & 7]

    barrier = pltpu.get_barrier_semaphore()
    for m in FAR_FIRST:
        pl.semaphore_signal(barrier, inc=1, device_id=(peer(m),), device_id_type=MESH)

    ph1 = (ph1a, ph1b, ph1c, ph1d)
    loads[0].wait()
    loads[1].wait()
    for i in range(CH):
        ph1[i // PR][0:OWN, i % PR, :] = control[:, i * 128:(i + 1) * 128]
    for k in range(NB):
        for c in range(4):
            part = cells[0, k:k + 1, c * 128:(c + 1) * 128]
            row16[4 * k + c:4 * k + c + 1, :] = lax.div(part, COLS)
            col16[4 * k + c:4 * k + c + 1, :] = lax.rem(part, COLS)
    up = lax.broadcasted_iota(jnp.int32, (ROWS, 128), 0)
    across = lax.broadcasted_iota(jnp.int32, (128, 128), 1)
    tall = lax.broadcasted_iota(jnp.int32, (COLS, 128), 0)
    for j in range(CH):
        pick[:, j * 128:(j + 1) * 128] = jnp.where(
            tall == col16[j:j + 1, :], 1.0, 0.0
        ).astype(BF16)
    nbr = [nbrs[k, me] for k in range(NB)]
    at = [differ(nbr[k], me, 7) for k in range(NB)]
    landing = (rbuf0, rbuf1)
    for buf in landing:
        buf[0] = jnp.zeros((4, 128), F32)

    def find_slot(q, carry):
        last = jnp.where(nbr[2] == q, 2, jnp.where(nbr[3] == q, 3, 0))
        kid[q] = jnp.where(nbr[1] == q, 1, last)
        return carry

    lax.fori_loop(0, NDEV, find_slot, 0)

    def take(field, out):
        high, low = halves(field)
        both = jnp.concatenate([high.astype(BF16), low.astype(BF16)], axis=0)
        for jj in range(CH // 2):
            lifted = dot(both, pick[:, jj * 256:(jj + 1) * 256])
            lifted = lifted[:ROWS] + lifted[ROWS:]
            for h in range(2):
                j = 2 * jj + h
                mine = jnp.where(
                    up == row16[j:j + 1, :], lifted[:, h * 128:(h + 1) * 128], 0.0
                )
                out[j:j + 1, :] = jnp.sum(mine, axis=0, keepdims=True)

    def put(values):
        high, low = halves(values)
        for j in range(CH):
            at_row = up == row16[j:j + 1, :]
            spread[0:ROWS, j * 128:(j + 1) * 128] = jnp.where(
                at_row, high[j:j + 1, :], 0.0
            ).astype(BF16)
            spread[ROWS:2 * ROWS, j * 128:(j + 1) * 128] = jnp.where(
                at_row, low[j:j + 1, :], 0.0
            ).astype(BF16)
        placed = dot(spread[...], pickt[...])
        return placed[:ROWS] + placed[ROWS:]

    few = lax.broadcasted_iota(jnp.int32, (CH, 128), 0)

    def same_cell(values):
        high, low = halves(values)
        mine = [few == uhi16[j:j + 1, :] for j in range(CH)]
        spread_h = [jnp.where(mine[j], high[j:j + 1, :], 0.0) for j in range(CH)]
        spread_l = [jnp.where(mine[j], low[j:j + 1, :], 0.0) for j in range(CH)]
        both = jnp.concatenate(
            [jnp.concatenate(spread_h, axis=1), jnp.concatenate(spread_l, axis=1)], axis=0
        ).astype(BF16)
        table = dot(both, uone[...])
        table = table[:CH] + table[CH:]
        uhi, ulo = uhi16[...], ulo16[...]
        out = jnp.zeros((CH, 128), F32)
        for r in range(CH):
            row = jnp.broadcast_to(table[r:r + 1, :], (CH, 128))
            found = jnp.take_along_axis(row, ulo, axis=1, mode="promise_in_bounds")
            out = jnp.where(uhi == r, found, out)
        return out

    def send(values, parity):
        for k in range(NB):
            fx[k] = values[4 * k:4 * k + 4, :]
        for m in FAR_FIRST:
            there = peer(m)
            sbuf[m - 1] = fx[kid[there]]
            pltpu.make_async_remote_copy(
                sbuf.at[m - 1], landing[parity].at[m], ssem, rsem.at[parity],
                device_id=(there,), device_id_type=MESH,
            ).start()

    def receive(parity):
        whole = pltpu.make_async_remote_copy(
            sbuf, landing[parity].at[pl.ds(1, NDEV - 1)], ssem, rsem.at[parity],
            device_id=(peer(1),), device_id_type=MESH,
        )
        whole.wait_recv()
        for k in range(NB):
            gx[4 * k:4 * k + 4, :] = landing[parity][at[k]]
        whole.wait_send()

    def wait_all(sent, arrived, size, count, send_sem, recv_sem):
        pltpu.make_async_remote_copy(
            sent.at[pl.ds(size, size * count)], arrived.at[pl.ds(size, size * count)],
            send_sem, recv_sem, device_id=(peer(1),), device_id_type=MESH,
        ).wait()

    def patch(v):
        right = wr[...] * (v - pltpu.roll(v, COLS - 1, 1))
        down = wd[...] * (v - pltpu.roll(v, ROWS - 1, 0))
        return right - pltpu.roll(right, 1, 1) + down - pltpu.roll(down, 1, 0)

    def unfold(ref, c):
        return ref[pl.ds(c, ROWS, stride=4), :]

    def grid(ref):
        return jnp.concatenate([unfold(ref, c) for c in range(4)], axis=1)

    loads[2].wait()
    h = grid(depth)
    take(h, xg)

    pl.semaphore_wait(barrier, NDEV - 1)

    for c in range(PIECES):
        for m in range(1, LOW):
            pltpu.make_async_remote_copy(
                ph1[c].at[pl.ds(0, OWN)], ph1[c].at[pl.ds(m * OWN, OWN)],
                s1.at[c], r1.at[c], device_id=(peer(m),), device_id_type=MESH,
            ).start()
    send(xg[...], 1)

    last_col = lax.broadcasted_iota(jnp.int32, (ROWS, COLS), 1) == COLS - 1
    last_row = lax.broadcasted_iota(jnp.int32, (ROWS, COLS), 0) == ROWS - 1
    wr[...] = jnp.where(last_col, 0.0, 0.5 * (h + pltpu.roll(h, COLS - 1, 1)))
    wd[...] = jnp.where(last_row, 0.0, 0.5 * (h + pltpu.roll(h, ROWS - 1, 0)))
    loads[3].wait()
    mask = grid(wet).astype(F32)
    kw[...] = KAPPA * mask
    take(mask, kwj)
    kwj[...] = KAPPA * kwj[...]
    for load in loads[4:]:
        load.wait()
    wgt[...] = kw[...] * grid(obs)
    take(wgt[...], obj)

    mins[...] = jnp.full((CH * 8, 128), 4096.0, F32)

    def earliest(i, carry):
        mine = row16[pl.ds(i, 1), :] * COLS + col16[pl.ds(i, 1), :]
        column = jnp.transpose(jnp.broadcast_to(mine.astype(F32), (128, 128)))
        number = (up + i * 128).astype(F32)
        for j in range(CH):
            other = (row16[j:j + 1, :] * COLS + col16[j:j + 1, :]).astype(F32)
            found = jnp.where(column == other, number, 4096.0)
            found = jnp.min(found.reshape(16, 8, 128), axis=0)
            mins[8 * j:8 * j + 8, :] = jnp.minimum(mins[8 * j:8 * j + 8, :], found)
        return carry

    lax.fori_loop(0, CH, earliest, 0)
    for j in range(CH):
        u = jnp.min(mins[8 * j:8 * j + 8, :], axis=0, keepdims=True).astype(jnp.int32)
        uhi16[j:j + 1, :] = lax.div(u, 128)
        ulo16[j:j + 1, :] = lax.rem(u, 128)
    for j in range(CH):
        ulo = ulo16[j:j + 1, :]
        column = jnp.transpose(jnp.broadcast_to(ulo.astype(F32), (128, 128)))
        uone[j * 128:(j + 1) * 128, :] = jnp.where(
            column == across.astype(F32), 1.0, 0.0
        ).astype(BF16)
        column = jnp.transpose(
            jnp.broadcast_to(col16[j:j + 1, :].astype(F32), (128, 128))
        )
        for c in range(4):
            pickt[j * 128:(j + 1) * 128, c * 128:(c + 1) * 128] = jnp.where(
                column == (across + c * 128).astype(F32), 1.0, 0.0
            ).astype(BF16)

    place = []
    for j in range(HIGHN):
        for k in range(READS):
            b = reads[k, high_of[j] + my_low]
            owner = lax.div(b, OWN)
            place.append(differ(lax.rem(owner, LOW), my_low, 3) * OWN + lax.rem(b, OWN))
    for c in range(PIECES):
        wait_all(ph1[c], ph1[c], OWN, LOW - 1, s1.at[c], r1.at[c])
        for j in range(HIGHN):
            part = pl.ds(j * READS, READS)
            goal = sb2 if j else rb2
            for k in range(READS):
                goal[c, j * READS + k] = ph1[c][place[j * READS + k]]
            if j:
                pltpu.make_async_remote_copy(
                    sb2.at[c, part], rb2.at[c, part], s2.at[c], r2.at[c],
                    device_id=(high_of[j] + my_low,), device_id_type=MESH,
                ).start()

    receive(1)
    ew[...] = 0.5 * (xg[...] + gx[...])
    dia[...] = put(ew[...])
    for r in range(READS):
        for p in range(2):
            at_row = (2 * r + p) * CH
            uall[at_row:at_row + CH, :] = brows[0, r, pl.ds(p, CH, stride=2), :]
    for c in range(PIECES):
        wait_all(sb2.at[c], rb2.at[c], READS, HIGHN - 1, s2.at[c], r2.at[c])

    lane16 = lax.broadcasted_iota(jnp.int32, (CH, 128), 1)
    zero = jnp.zeros((2 * CH, 128), F32)
    diagonal = []
    for k in range(READS):
        owner = lax.div(reads[k, me], OWN)
        row = differ(lax.div(owner, LOW), my_high, 4)
        block = jnp.concatenate(
            [rb2[c, row * READS + k] for c in range(PIECES)], axis=0
        )
        turned = pltpu.roll(block, 64, 1)
        if k % 2:
            both = [jnp.where(lane16 < 64, 0.0, v) for v in (turned, block)]
        else:
            both = [jnp.where(lane16 < 64, v, 0.0) for v in (block, turned)]
        both = jnp.concatenate(both, axis=0)
        diagonal.append(jnp.concatenate([zero, both] if k > 1 else [both, zero], axis=1))
    uy = bcols[0].reshape(READS * 64, COLS)
    inner = dot(jnp.concatenate(diagonal, axis=0), uy, HIGH)
    bathy = dot(jnp.transpose(uall[...]), inner, HIGH)
    src[...] = kw[...] * grid(sens) * bathy

    bgr[...] = src[...]
    take(src[...], pg)
    gx[...] = jnp.zeros((CH, 128), F32)

    def step(n, parity):
        send(pg[...], parity)
        k = kw[...]
        e = bgr[...] + k * put(gx[...])
        turn = n == TURN
        s = jnp.where(turn, wgt[...] * e, src[...])
        seen[...] = jnp.where(turn, e, seen[...])
        e = jnp.where(turn, s, e)
        src[...] = s
        new = e - k * (patch(e) + dia[...] * e) + s
        bgr[...] = new
        ahead = n == TURN - 1
        take(jnp.where(ahead, wgt[...] * new, new), pg)
        receive(parity)
        x = ew[...] * gx[...]
        gx[...] = x
        scale = jnp.where(ahead, obj[...] * kwj[...], kwj[...])
        pg[...] = pg[...] + scale * same_cell(x)

    def pair(i, carry):
        step(2 * i, 0)
        step(2 * i + 1, 1)
        return carry

    seen[...] = src[...]
    lax.fori_loop(0, TURN, pair, 0)
    last = bgr[...] + kw[...] * put(gx[...])
    seen_obs = grid(obs) * seen[...]
    for c in range(4):
        wobs[pl.ds(c, ROWS, stride=4), :] = seen_obs[:, c * 128:(c + 1) * 128]

    grad = grid(sens) * last
    side = dot(uall[...], grad, HIGH)
    full = lax.dot_general(
        side, bcols[0].reshape(READS * 64, COLS), (((1,), (1,)), ((), ())),
        precision=HIGH, preferred_element_type=F32,
    )
    for r in range(READS):
        half = full[:, (r // 2) * 128:(r // 2 + 1) * 128]
        even = half[2 * r * CH:(2 * r + 1) * CH]
        odd = half[(2 * r + 1) * CH:(2 * r + 2) * CH]
        if r % 2:
            even = pltpu.roll(even, 64, 1)
        else:
            odd = pltpu.roll(odd, 64, 1)
        block = jnp.where(lane16 < 64, even, odd)
        for c in range(PIECES):
            gr[c, r] = block[c * PR:(c + 1) * PR]

    for c in range(PIECES):
        for j in range(1, HIGHN):
            pltpu.make_async_remote_copy(
                gr.at[c, pl.ds(0, READS)], gr.at[c, pl.ds(j * READS, READS)],
                s3.at[c], r3.at[c],
                device_id=(high_of[j] + my_low,), device_id_type=MESH,
            ).start()
    lane = lax.broadcasted_iota(jnp.int32, (1, 128), 1)
    wt[...] = jnp.zeros((128, 128), F32)
    for j in range(HIGHN):
        for k in range(READS):
            s = j * READS + k
            owner = lax.div(reads[k, high_of[j] + my_low], OWN)
            index = jnp.where(lax.div(owner, LOW) == my_high, place[s], -1)
            wt[s:s + 1, :] = jnp.where(lane == index, 1.0, 0.0)
    gather = jnp.transpose(wt[...])[:64, :64]
    for c in range(PIECES):
        wait_all(gr.at[c], gr.at[c], READS, HIGHN - 1, s3.at[c], r3.at[c])
        for i in range(PR):
            sp[c, :, i, :] = dot(gather, gr[c, :, i, :], HIGH)
        for m in range(1, LOW):
            part = pl.ds(m * OWN, OWN)
            pltpu.make_async_remote_copy(
                sp.at[c, part], rp.at[c, part], s4.at[c], r4.at[c],
                device_id=(peer(m),), device_id_type=MESH,
            ).start()
    for c in range(PIECES):
        wait_all(sp.at[c], rp.at[c], OWN, LOW - 1, s4.at[c], r4.at[c])
        total = sp[c, 0:OWN]
        for m in range(1, LOW):
            total = total + rp[c, m * OWN:(m + 1) * OWN]
        acc[c] = total
        for i in range(PR):
            at_lane = (c * PR + i) * 128
            hess[:, at_lane:at_lane + 128] = acc[c, :, i, :]


def on_device(
    control, reads, neighbours, halo_cells, wet_mask, depth, sensitivity, obs_weight,
    basis_rows, basis_cols,
):
    flat = (ROWS * COLS // 128, 128)
    field = pltpu.VMEM((ROWS, COLS), F32)
    few = pltpu.VMEM((CH, 128), F32)
    few_int = pltpu.VMEM((CH, 128), jnp.int32)
    edges = CH * 128
    blocks = pltpu.VMEM((PIECES, LOW * OWN, PR, 128), F32)
    dma = pltpu.SemaphoreType.DMA
    vmem = pl.BlockSpec(memory_space=pltpu.VMEM)
    hess, wobs = pl.pallas_call(
        kernel,
        name="hessian_product",
        out_shape=(
            jax.ShapeDtypeStruct(control.shape, F32),
            jax.ShapeDtypeStruct(flat, F32),
        ),
        in_specs=[pl.BlockSpec(memory_space=pltpu.SMEM)] * 2
        + [pl.BlockSpec(memory_space=pltpu.HBM)] * 8,
        out_specs=(vmem, vmem),
        scratch_shapes=[
            pltpu.VMEM(control.shape, F32),
            pltpu.VMEM(halo_cells.shape, jnp.int32),
            pltpu.VMEM(flat, jnp.int32),
            pltpu.VMEM(flat, F32),
            pltpu.VMEM(flat, F32),
            pltpu.VMEM(flat, F32),
            pltpu.VMEM(basis_rows.shape, F32),
            pltpu.VMEM(basis_cols.shape, F32),
            dma((8,)),
            field, field, field, field, field, field, field,
            few,
            field,
            pltpu.VMEM((COLS, edges), BF16),
            pltpu.VMEM((edges, COLS), BF16),
            pltpu.VMEM((2 * ROWS, edges), BF16),
            pltpu.VMEM((edges, 128), BF16),
            few_int, few_int, few_int, few_int,
            pltpu.VMEM((CH * 8, 128), F32),
            few, few, few, few,
            pltpu.VMEM((NB, 4, 128), F32),
            few,
            pltpu.VMEM((NDEV - 1, 4, 128), F32),
            pltpu.VMEM((NDEV, 4, 128), F32),
            pltpu.VMEM((NDEV, 4, 128), F32),
            *[pltpu.VMEM((LOW * OWN, PR, 128), F32) for _ in range(PIECES)],
            blocks, blocks, blocks, blocks, blocks,
            pltpu.VMEM((128, 128), F32),
            pltpu.VMEM((128, 128), F32),
            pltpu.VMEM((PIECES, OWN, PR, 128), F32),
            pltpu.SMEM((NDEV,), jnp.int32),
            dma, dma((2,)),
            *[dma((PIECES,)) for _ in range(8)],
        ],
        compiler_params=pltpu.CompilerParams(
            collective_id=0, has_side_effects=True, vmem_limit_bytes=63 << 20
        ),
    )(
        reads.T, neighbours.T, control, halo_cells, wet_mask.reshape(flat), depth.reshape(flat),
        sensitivity.reshape(flat), obs_weight.reshape(flat), basis_rows, basis_cols,
    )
    return hess, wobs.reshape(-1)


def solution(mesh):
    return jax.shard_map(
        on_device,
        mesh=mesh,
        in_specs=(
            P("dom", None), P(), P(), P("dom", None, None), P("dom"), P("dom"), P("dom"),
            P("dom"), P("dom", None, None, None), P("dom", None, None, None),
        ),
        out_specs=(P("dom", None), P("dom")),
        check_vma=False,
    )
```

```python
import random

import jax
import jax.numpy as jnp
from jax import lax
from jax.experimental import pallas as pl
from jax.experimental.pallas import tpu as pltpu
from jax.sharding import PartitionSpec as P

STEPS = 12
TURN = STEPS - 1
KAPPA = 0.11
HIGH = lax.Precision.HIGHEST
MESH = pl.DeviceIdType.MESH
F32 = jnp.float32
BF16 = jnp.bfloat16

NDEV = 128
LOW = 8
HIGHN = 16
ROWS, COLS = 128, 512
NB, READS, OWN = 4, 4, 8
PIECES = 4
CH = 16
PR = CH // PIECES


def ring(d):
    return (0, 1, 2, 1)[d]


def hops(m):
    return ring((m >> 1) & 3) + ring((m >> 3) & 3) + ring((m >> 5) & 3)


def far_first():
    order = list(range(1, NDEV))
    random.Random(1).shuffle(order)
    return sorted(order, key=lambda m: -hops(m))


FAR_FIRST = far_first()


def flip(value, mask, bits):
    out = value
    for i in range(bits):
        if (mask >> i) & 1:
            bit = lax.rem(lax.div(value, 1 << i), 2)
            out = out + (1 - 2 * bit) * (1 << i)
    return out


def differ(a, b, bits):
    out = 0
    for i in range(bits):
        d = lax.rem(lax.div(a, 1 << i), 2) - lax.rem(lax.div(b, 1 << i), 2)
        out = out + d * d * (1 << i)
    return out


def dot(a, b, precision=None):
    return jnp.dot(a, b, precision=precision, preferred_element_type=F32)


def halves(v):
    high = v.astype(BF16).astype(F32)
    return high, v - high


def kernel(
    reads, nbrs, control_hbm, cells_hbm, wet_hbm, depth_hbm, sens_hbm, obs_hbm,
    brows_hbm, bcols_hbm,
    hess, wobs_hbm,
    wobs, outsem,
    control, cells, wet, depth, sens, obs, brows, bcols, insem,
    kw, wr, wd, dia, src, bgr, wgt, obj, seen, pick, pickt, spread, uone,
    row16, col16, uhi16, ulo16, mins, ew, kwj, xg, gx, fx, pg, sbuf, rbuf0, rbuf1, rbuf2,
    ph1a, ph1b, ph1c, ph1d, sb2, rb2, gr, sp, rp, wt, uall, acc, kid,
    ssem, rsem, s1, r1, s2, r2, s3, r3, s4, r4,
):
    names = (control, cells, depth, wet, brows, bcols, sens, obs)
    sources = (
        control_hbm, cells_hbm, depth_hbm, wet_hbm, brows_hbm, bcols_hbm, sens_hbm, obs_hbm
    )
    loads = [
        pltpu.make_async_copy(a, b, insem.at[i])
        for i, (a, b) in enumerate(zip(sources, names))
    ]
    for load in loads:
        load.start()
    me = lax.axis_index("dom")
    my_low = lax.rem(me, LOW)
    my_high = lax.div(me, LOW)
    low_of = [flip(my_low, m, 3) for m in range(LOW)]
    high_of = [flip(my_high, m, 4) * LOW for m in range(HIGHN)]

    def peer(m):
        return high_of[m >> 3] + low_of[m & 7]

    barrier = pltpu.get_barrier_semaphore()
    for m in FAR_FIRST:
        pl.semaphore_signal(barrier, inc=1, device_id=(peer(m),), device_id_type=MESH)

    ph1 = (ph1a, ph1b, ph1c, ph1d)
    loads[0].wait()
    for i in range(CH):
        ph1[i // PR][0:OWN, i % PR, :] = control[:, i * 128:(i + 1) * 128]
    loads[1].wait()
    for k in range(NB):
        for c in range(4):
            part = cells[0, k:k + 1, c * 128:(c + 1) * 128]
            row16[4 * k + c:4 * k + c + 1, :] = lax.div(part, COLS)
            col16[4 * k + c:4 * k + c + 1, :] = lax.rem(part, COLS)
    up = lax.broadcasted_iota(jnp.int32, (ROWS, 128), 0)
    across = lax.broadcasted_iota(jnp.int32, (128, 128), 1)
    tall = lax.broadcasted_iota(jnp.int32, (COLS, 128), 0)
    for j in range(CH):
        pick[:, j * 128:(j + 1) * 128] = jnp.where(
            tall == col16[j:j + 1, :], 1.0, 0.0
        ).astype(BF16)
    nbr = [nbrs[k, me] for k in range(NB)]
    at = [differ(nbr[k], me, 7) for k in range(NB)]
    landing = (rbuf0, rbuf1, rbuf2)
    for buf in landing:
        buf[0] = jnp.zeros((4, 128), F32)

    def find_slot(q, carry):
        last = jnp.where(nbr[2] == q, 2, jnp.where(nbr[3] == q, 3, 0))
        kid[q] = jnp.where(nbr[1] == q, 1, last)
        return carry

    lax.fori_loop(0, NDEV, find_slot, 0)

    def take(field, out):
        high, low = halves(field)
        both = jnp.concatenate([high.astype(BF16), low.astype(BF16)], axis=0)
        for jj in range(CH // 2):
            lifted = dot(both, pick[:, jj * 256:(jj + 1) * 256])
            lifted = lifted[:ROWS] + lifted[ROWS:]
            for h in range(2):
                j = 2 * jj + h
                mine = jnp.where(
                    up == row16[j:j + 1, :], lifted[:, h * 128:(h + 1) * 128], 0.0
                )
                out[j:j + 1, :] = jnp.sum(mine, axis=0, keepdims=True)

    def put(values):
        high, low = halves(values)
        for j in range(CH):
            at_row = up == row16[j:j + 1, :]
            spread[0:ROWS, j * 128:(j + 1) * 128] = jnp.where(
                at_row, high[j:j + 1, :], 0.0
            ).astype(BF16)
            spread[ROWS:2 * ROWS, j * 128:(j + 1) * 128] = jnp.where(
                at_row, low[j:j + 1, :], 0.0
            ).astype(BF16)
        placed = dot(spread[...], pickt[...])
        return placed[:ROWS] + placed[ROWS:]

    few = lax.broadcasted_iota(jnp.int32, (CH, 128), 0)

    def same_cell(values):
        high, low = halves(values)
        mine = [few == uhi16[j:j + 1, :] for j in range(CH)]
        spread_h = [jnp.where(mine[j], high[j:j + 1, :], 0.0) for j in range(CH)]
        spread_l = [jnp.where(mine[j], low[j:j + 1, :], 0.0) for j in range(CH)]
        both = jnp.concatenate(
            [jnp.concatenate(spread_h, axis=1), jnp.concatenate(spread_l, axis=1)], axis=0
        ).astype(BF16)
        table = dot(both, uone[...])
        table = table[:CH] + table[CH:]
        uhi, ulo = uhi16[...], ulo16[...]
        out = jnp.zeros((CH, 128), F32)
        for r in range(CH):
            row = jnp.broadcast_to(table[r:r + 1, :], (CH, 128))
            found = jnp.take_along_axis(row, ulo, axis=1, mode="promise_in_bounds")
            out = jnp.where(uhi == r, found, out)
        return out

    def stage(values):
        for k in range(NB):
            fx[k] = values[4 * k:4 * k + 4, :]

    def send(parity):
        for m in FAR_FIRST:
            there = peer(m)
            sbuf[m - 1] = fx[kid[there]]
            pltpu.make_async_remote_copy(
                sbuf.at[m - 1], landing[parity].at[m], ssem, rsem.at[parity],
                device_id=(there,), device_id_type=MESH,
            ).start()

    def receive(parity):
        whole = pltpu.make_async_remote_copy(
            sbuf, landing[parity].at[pl.ds(1, NDEV - 1)], ssem, rsem.at[parity],
            device_id=(peer(1),), device_id_type=MESH,
        )
        whole.wait_recv()
        for k in range(NB):
            gx[4 * k:4 * k + 4, :] = landing[parity][at[k]]
        if parity < 2:
            whole.wait_send()

    def wait_all(sent, arrived, size, count, send_sem, recv_sem):
        pltpu.make_async_remote_copy(
            sent.at[pl.ds(size, size * count)], arrived.at[pl.ds(size, size * count)],
            send_sem, recv_sem, device_id=(peer(1),), device_id_type=MESH,
        ).wait()

    def patch(v):
        right = wr[...] * (v - pltpu.roll(v, COLS - 1, 1))
        down = wd[...] * (v - pltpu.roll(v, ROWS - 1, 0))
        return right - pltpu.roll(right, 1, 1) + down - pltpu.roll(down, 1, 0)

    def unfold(ref, c):
        return ref[pl.ds(c, ROWS, stride=4), :]

    def grid(ref):
        return jnp.concatenate([unfold(ref, c) for c in range(4)], axis=1)

    loads[2].wait()
    h = grid(depth)
    take(h, xg)

    place = []
    for j in range(HIGHN):
        for k in range(READS):
            b = reads[k, high_of[j] + my_low]
            owner = lax.div(b, OWN)
            place.append(differ(lax.rem(owner, LOW), my_low, 3) * OWN + lax.rem(b, OWN))
    pl.semaphore_wait(barrier, NDEV - 1)

    for c in range(PIECES):
        for m in range(1, LOW):
            pltpu.make_async_remote_copy(
                ph1[c].at[pl.ds(0, OWN)], ph1[c].at[pl.ds(m * OWN, OWN)],
                s1.at[c], r1.at[c], device_id=(peer(m),), device_id_type=MESH,
            ).start()
    last_col = lax.broadcasted_iota(jnp.int32, (ROWS, COLS), 1) == COLS - 1
    last_row = lax.broadcasted_iota(jnp.int32, (ROWS, COLS), 0) == ROWS - 1
    wr[...] = jnp.where(last_col, 0.0, 0.5 * (h + pltpu.roll(h, COLS - 1, 1)))
    wd[...] = jnp.where(last_row, 0.0, 0.5 * (h + pltpu.roll(h, ROWS - 1, 0)))
    loads[3].wait()
    mask = grid(wet).astype(F32)
    kw[...] = KAPPA * mask
    take(mask, kwj)
    kwj[...] = KAPPA * kwj[...]
    for c in range(PIECES):
        wait_all(ph1[c], ph1[c], OWN, LOW - 1, s1.at[c], r1.at[c])
        for j in range(HIGHN):
            part = pl.ds(j * READS, READS)
            goal = sb2 if j else rb2
            for k in range(READS):
                goal[c, j * READS + k] = ph1[c][place[j * READS + k]]
            if j:
                pltpu.make_async_remote_copy(
                    sb2.at[c, part], rb2.at[c, part], s2.at[c], r2.at[c],
                    device_id=(high_of[j] + my_low,), device_id_type=MESH,
                ).start()

    stage(xg[...])
    send(2)

    for load in loads[4:]:
        load.wait()
    wgt[...] = kw[...] * grid(obs)
    take(wgt[...], obj)

    mins[...] = jnp.full((CH * 8, 128), 4096.0, F32)

    def earliest(i, carry):
        mine = row16[pl.ds(i, 1), :] * COLS + col16[pl.ds(i, 1), :]
        column = jnp.transpose(jnp.broadcast_to(mine.astype(F32), (128, 128)))
        number = (up + i * 128).astype(F32)
        for j in range(CH):
            other = (row16[j:j + 1, :] * COLS + col16[j:j + 1, :]).astype(F32)
            found = jnp.where(column == other, number, 4096.0)
            found = jnp.min(found.reshape(16, 8, 128), axis=0)
            mins[8 * j:8 * j + 8, :] = jnp.minimum(mins[8 * j:8 * j + 8, :], found)
        return carry

    lax.fori_loop(0, CH, earliest, 0)
    for j in range(CH):
        u = jnp.min(mins[8 * j:8 * j + 8, :], axis=0, keepdims=True).astype(jnp.int32)
        uhi16[j:j + 1, :] = lax.div(u, 128)
        ulo16[j:j + 1, :] = lax.rem(u, 128)
    for j in range(CH):
        ulo = ulo16[j:j + 1, :]
        column = jnp.transpose(jnp.broadcast_to(ulo.astype(F32), (128, 128)))
        uone[j * 128:(j + 1) * 128, :] = jnp.where(
            column == across.astype(F32), 1.0, 0.0
        ).astype(BF16)
        column = jnp.transpose(
            jnp.broadcast_to(col16[j:j + 1, :].astype(F32), (128, 128))
        )
        for c in range(4):
            pickt[j * 128:(j + 1) * 128, c * 128:(c + 1) * 128] = jnp.where(
                column == (across + c * 128).astype(F32), 1.0, 0.0
            ).astype(BF16)

    pltpu.make_async_remote_copy(
        sbuf, rbuf2.at[pl.ds(1, NDEV - 1)], ssem, rsem.at[2],
        device_id=(peer(1),), device_id_type=MESH,
    ).wait_send()
    for r in range(READS):
        for p in range(2):
            at_row = (2 * r + p) * CH
            uall[at_row:at_row + CH, :] = brows[0, r, pl.ds(p, CH, stride=2), :]
    for c in range(PIECES):
        wait_all(sb2.at[c], rb2.at[c], READS, HIGHN - 1, s2.at[c], r2.at[c])

    lane16 = lax.broadcasted_iota(jnp.int32, (CH, 128), 1)
    zero = jnp.zeros((2 * CH, 128), F32)
    diagonal = []
    for k in range(READS):
        owner = lax.div(reads[k, me], OWN)
        row = differ(lax.div(owner, LOW), my_high, 4)
        block = jnp.concatenate(
            [rb2[c, row * READS + k] for c in range(PIECES)], axis=0
        )
        turned = pltpu.roll(block, 64, 1)
        if k % 2:
            both = [jnp.where(lane16 < 64, 0.0, v) for v in (turned, block)]
        else:
            both = [jnp.where(lane16 < 64, v, 0.0) for v in (block, turned)]
        both = jnp.concatenate(both, axis=0)
        diagonal.append(jnp.concatenate([zero, both] if k > 1 else [both, zero], axis=1))
    uy = bcols[0].reshape(READS * 64, COLS)
    inner = dot(jnp.concatenate(diagonal, axis=0), uy, HIGH)
    bathy = dot(jnp.transpose(uall[...]), inner, HIGH)
    src[...] = kw[...] * grid(sens) * bathy

    bgr[...] = src[...]
    take(src[...], pg)
    gx[...] = jnp.zeros((CH, 128), F32)

    def step(n, parity):
        stage(pg[...])
        send(parity)
        if parity == 0:
            @pl.when(n == 0)
            def _():
                receive(2)
                ew[...] = 0.5 * (xg[...] + gx[...])
                dia[...] = put(ew[...])
                gx[...] = jnp.zeros((CH, 128), F32)

        k = kw[...]
        e = bgr[...] + k * put(gx[...])
        turn = n == TURN
        s = jnp.where(turn, wgt[...] * e, src[...])
        seen[...] = jnp.where(turn, e, seen[...])
        e = jnp.where(turn, s, e)
        src[...] = s
        new = e - k * (patch(e) + dia[...] * e) + s
        bgr[...] = new
        ahead = n == TURN - 1
        take(jnp.where(ahead, wgt[...] * new, new), pg)
        receive(parity)
        x = ew[...] * gx[...]
        gx[...] = x
        scale = jnp.where(ahead, obj[...] * kwj[...], kwj[...])
        pg[...] = pg[...] + scale * same_cell(x)

    def pair(i, carry):
        step(2 * i, 0)
        step(2 * i + 1, 1)
        return carry

    seen[...] = src[...]
    lax.fori_loop(0, TURN, pair, 0)
    last = bgr[...] + kw[...] * put(gx[...])
    seen_obs = grid(obs) * seen[...]
    for c in range(4):
        wobs[pl.ds(c, ROWS, stride=4), :] = seen_obs[:, c * 128:(c + 1) * 128]
    store = pltpu.make_async_copy(wobs, wobs_hbm, outsem)
    store.start()

    grad = grid(sens) * last
    side = dot(uall[...], grad, HIGH)
    full = lax.dot_general(
        side, bcols[0].reshape(READS * 64, COLS), (((1,), (1,)), ((), ())),
        precision=HIGH, preferred_element_type=F32,
    )
    for r in range(READS):
        half = full[:, (r // 2) * 128:(r // 2 + 1) * 128]
        even = half[2 * r * CH:(2 * r + 1) * CH]
        odd = half[(2 * r + 1) * CH:(2 * r + 2) * CH]
        if r % 2:
            even = pltpu.roll(even, 64, 1)
        else:
            odd = pltpu.roll(odd, 64, 1)
        block = jnp.where(lane16 < 64, even, odd)
        for c in range(PIECES):
            gr[c, r] = block[c * PR:(c + 1) * PR]

    for c in range(PIECES):
        for j in range(1, HIGHN):
            pltpu.make_async_remote_copy(
                gr.at[c, pl.ds(0, READS)], gr.at[c, pl.ds(j * READS, READS)],
                s3.at[c], r3.at[c],
                device_id=(high_of[j] + my_low,), device_id_type=MESH,
            ).start()
    lane = lax.broadcasted_iota(jnp.int32, (1, 128), 1)
    wt[...] = jnp.zeros((128, 128), F32)
    for j in range(HIGHN):
        for k in range(READS):
            s = j * READS + k
            owner = lax.div(reads[k, high_of[j] + my_low], OWN)
            index = jnp.where(lax.div(owner, LOW) == my_high, place[s], -1)
            wt[s:s + 1, :] = jnp.where(lane == index, 1.0, 0.0)
    gather = jnp.transpose(wt[...])[:64, :64]
    gather = jnp.concatenate([gather, gather], axis=1).astype(BF16)
    for c in range(PIECES):
        wait_all(gr.at[c], gr.at[c], READS, HIGHN - 1, s3.at[c], r3.at[c])
        wide = jnp.concatenate([gr[c, :, i, :] for i in range(PR)], axis=1)
        wide = dot(gather, jnp.concatenate(halves(wide), axis=0).astype(BF16))
        for i in range(PR):
            sp[c, :, i, :] = wide[:, i * 128:(i + 1) * 128]
        for m in range(1, LOW):
            part = pl.ds(m * OWN, OWN)
            pltpu.make_async_remote_copy(
                sp.at[c, part], rp.at[c, part], s4.at[c], r4.at[c],
                device_id=(peer(m),), device_id_type=MESH,
            ).start()
    for c in range(PIECES):
        wait_all(sp.at[c], rp.at[c], OWN, LOW - 1, s4.at[c], r4.at[c])
        total = sp[c, 0:OWN]
        for m in range(1, LOW):
            total = total + rp[c, m * OWN:(m + 1) * OWN]
        acc[c] = total
        for i in range(PR):
            at_lane = (c * PR + i) * 128
            hess[:, at_lane:at_lane + 128] = acc[c, :, i, :]
    store.wait()


def on_device(
    control, reads, neighbours, halo_cells, wet_mask, depth, sensitivity, obs_weight,
    basis_rows, basis_cols,
):
    flat = (ROWS * COLS // 128, 128)
    field = pltpu.VMEM((ROWS, COLS), F32)
    few = pltpu.VMEM((CH, 128), F32)
    few_int = pltpu.VMEM((CH, 128), jnp.int32)
    edges = CH * 128
    blocks = pltpu.VMEM((PIECES, LOW * OWN, PR, 128), F32)
    dma = pltpu.SemaphoreType.DMA
    vmem = pl.BlockSpec(memory_space=pltpu.VMEM)
    hess, wobs = pl.pallas_call(
        kernel,
        name="hessian_product",
        out_shape=(
            jax.ShapeDtypeStruct(control.shape, F32),
            jax.ShapeDtypeStruct(flat, F32),
        ),
        in_specs=[pl.BlockSpec(memory_space=pltpu.SMEM)] * 2
        + [pl.BlockSpec(memory_space=pltpu.HBM)] * 8,
        out_specs=(vmem, pl.BlockSpec(memory_space=pltpu.HBM)),
        scratch_shapes=[
            pltpu.VMEM(flat, F32),
            dma,
            pltpu.VMEM(control.shape, F32),
            pltpu.VMEM(halo_cells.shape, jnp.int32),
            pltpu.VMEM(flat, jnp.int32),
            pltpu.VMEM(flat, F32),
            pltpu.VMEM(flat, F32),
            pltpu.VMEM(flat, F32),
            pltpu.VMEM(basis_rows.shape, F32),
            pltpu.VMEM(basis_cols.shape, F32),
            dma((8,)),
            field, field, field, field, field, field, field,
            few,
            field,
            pltpu.VMEM((COLS, edges), BF16),
            pltpu.VMEM((edges, COLS), BF16),
            pltpu.VMEM((2 * ROWS, edges), BF16),
            pltpu.VMEM((edges, 128), BF16),
            few_int, few_int, few_int, few_int,
            pltpu.VMEM((CH * 8, 128), F32),
            few, few, few, few,
            pltpu.VMEM((NB, 4, 128), F32),
            few,
            pltpu.VMEM((NDEV - 1, 4, 128), F32),
            pltpu.VMEM((NDEV, 4, 128), F32),
            pltpu.VMEM((NDEV, 4, 128), F32),
            pltpu.VMEM((NDEV, 4, 128), F32),
            *[pltpu.VMEM((LOW * OWN, PR, 128), F32) for _ in range(PIECES)],
            blocks, blocks, blocks, blocks, blocks,
            pltpu.VMEM((128, 128), F32),
            pltpu.VMEM((128, 128), F32),
            pltpu.VMEM((PIECES, OWN, PR, 128), F32),
            pltpu.SMEM((NDEV,), jnp.int32),
            dma, dma((3,)),
            *[dma((PIECES,)) for _ in range(8)],
        ],
        compiler_params=pltpu.CompilerParams(
            collective_id=0, has_side_effects=True, vmem_limit_bytes=63 << 20
        ),
    )(
        reads.T, neighbours.T, control, halo_cells, wet_mask.reshape(flat), depth.reshape(flat),
        sensitivity.reshape(flat), obs_weight.reshape(flat), basis_rows, basis_cols,
    )
    return hess, wobs.reshape(-1)


def solution(mesh):
    return jax.shard_map(
        on_device,
        mesh=mesh,
        in_specs=(
            P("dom", None), P(), P(), P("dom", None, None), P("dom"), P("dom"), P("dom"),
            P("dom"), P("dom", None, None, None), P("dom", None, None, None),
        ),
        out_specs=(P("dom", None), P("dom")),
        check_vma=False,
    )
```

```python
import random

import jax
import jax.numpy as jnp
from jax import lax
from jax.experimental import pallas as pl
from jax.experimental.pallas import tpu as pltpu
from jax.sharding import PartitionSpec as P

STEPS = 12
TURN = STEPS - 1
KAPPA = 0.11
HIGH = lax.Precision.HIGHEST
MESH = pl.DeviceIdType.MESH
F32 = jnp.float32
BF16 = jnp.bfloat16

NDEV = 128
LOW = 8
HIGHN = 16
ROWS, COLS = 128, 512
NB, READS, OWN = 4, 4, 8
PIECES = 4
CH = 16
PR = CH // PIECES


def ring(d):
    return (0, 1, 2, 1)[d]


def hops(m):
    return ring((m >> 1) & 3) + ring((m >> 3) & 3) + ring((m >> 5) & 3)


def far_first():
    order = list(range(1, NDEV))
    random.Random(1).shuffle(order)
    return sorted(order, key=lambda m: -hops(m))


FAR_FIRST = far_first()


def flip(value, mask, bits):
    out = value
    for i in range(bits):
        if (mask >> i) & 1:
            bit = lax.rem(lax.div(value, 1 << i), 2)
            out = out + (1 - 2 * bit) * (1 << i)
    return out


ROLES = (0, 1, 2, 0)


def low_mask(axis, t):
    return (t & 1) | ((t >> 1) << (1 + 2 * axis))


def high_mask(axis, j):
    one, two = [b for b in range(3) if b != axis]
    return ((j & 3) << (1 + 2 * one)) | ((j >> 2) << (1 + 2 * two))


def place_on(axis, d):
    return lax.rem(lax.div(d, 2 * 4 ** axis), 4)


def low_index(axis, d):
    return lax.rem(d, 2) + 2 * place_on(axis, d)


def high_index(axis, d):
    one, two = [b for b in range(3) if b != axis]
    return place_on(one, d) + 4 * place_on(two, d)


def differ(a, b, bits):
    out = 0
    for i in range(bits):
        d = lax.rem(lax.div(a, 1 << i), 2) - lax.rem(lax.div(b, 1 << i), 2)
        out = out + d * d * (1 << i)
    return out


def dot(a, b, precision=None):
    return jnp.dot(a, b, precision=precision, preferred_element_type=F32)


def halves(v):
    high = v.astype(BF16).astype(F32)
    return high, v - high


def kernel(
    reads, nbrs, control_hbm, cells_hbm, wet_hbm, depth_hbm, sens_hbm, obs_hbm,
    brows_hbm, bcols_hbm,
    hess, wobs_hbm,
    wobs, outsem,
    control, cells, wet, depth, sens, obs, brows, bcols, insem,
    kw, wr, wd, dia, src, bgr, wgt, obj, seen, pick, pickt, spread, uone,
    row16, col16, uhi16, ulo16, mins, ew, kwj, xg, gx, fx, pg, sbuf, rbuf0, rbuf1, rbuf2,
    ph1a, ph1b, ph1c, ph1d, sb2, rb2, gr, sp, rp, wt, uall, acc, kid,
    ssem, rsem, s1, r1, s2, r2, s3, r3, s4, r4,
):
    names = (control, cells, depth, wet, brows, bcols, sens, obs)
    sources = (
        control_hbm, cells_hbm, depth_hbm, wet_hbm, brows_hbm, bcols_hbm, sens_hbm, obs_hbm
    )
    loads = [
        pltpu.make_async_copy(a, b, insem.at[i])
        for i, (a, b) in enumerate(zip(sources, names))
    ]
    for load in loads:
        load.start()
    me = lax.axis_index("dom")
    my_low = lax.rem(me, LOW)
    my_high = lax.div(me, LOW)
    low_of = [flip(my_low, m, 3) for m in range(LOW)]
    high_of = [flip(my_high, m, 4) * LOW for m in range(HIGHN)]

    def peer(m):
        return high_of[m >> 3] + low_of[m & 7]

    barrier = pltpu.get_barrier_semaphore()
    for m in FAR_FIRST:
        pl.semaphore_signal(barrier, inc=1, device_id=(peer(m),), device_id_type=MESH)

    ph1 = (ph1a, ph1b, ph1c, ph1d)
    loads[0].wait()
    for i in range(CH):
        ph1[i // PR][0:OWN, i % PR, :] = control[:, i * 128:(i + 1) * 128]
    loads[1].wait()
    for k in range(NB):
        for c in range(4):
            part = cells[0, k:k + 1, c * 128:(c + 1) * 128]
            row16[4 * k + c:4 * k + c + 1, :] = lax.div(part, COLS)
            col16[4 * k + c:4 * k + c + 1, :] = lax.rem(part, COLS)
    up = lax.broadcasted_iota(jnp.int32, (ROWS, 128), 0)
    across = lax.broadcasted_iota(jnp.int32, (128, 128), 1)
    tall = lax.broadcasted_iota(jnp.int32, (COLS, 128), 0)
    for j in range(CH):
        pick[:, j * 128:(j + 1) * 128] = jnp.where(
            tall == col16[j:j + 1, :], 1.0, 0.0
        ).astype(BF16)
    nbr = [nbrs[k, me] for k in range(NB)]
    at = [differ(nbr[k], me, 7) for k in range(NB)]
    landing = (rbuf0, rbuf1, rbuf2)
    for buf in landing:
        buf[0] = jnp.zeros((4, 128), F32)

    def find_slot(q, carry):
        last = jnp.where(nbr[2] == q, 2, jnp.where(nbr[3] == q, 3, 0))
        kid[q] = jnp.where(nbr[1] == q, 1, last)
        return carry

    lax.fori_loop(0, NDEV, find_slot, 0)

    def take(field, out):
        high, low = halves(field)
        both = jnp.concatenate([high.astype(BF16), low.astype(BF16)], axis=0)
        for jj in range(CH // 2):
            lifted = dot(both, pick[:, jj * 256:(jj + 1) * 256])
            lifted = lifted[:ROWS] + lifted[ROWS:]
            for h in range(2):
                j = 2 * jj + h
                mine = jnp.where(
                    up == row16[j:j + 1, :], lifted[:, h * 128:(h + 1) * 128], 0.0
                )
                out[j:j + 1, :] = jnp.sum(mine, axis=0, keepdims=True)

    def put(values):
        high, low = halves(values)
        for j in range(CH):
            at_row = up == row16[j:j + 1, :]
            spread[0:ROWS, j * 128:(j + 1) * 128] = jnp.where(
                at_row, high[j:j + 1, :], 0.0
            ).astype(BF16)
            spread[ROWS:2 * ROWS, j * 128:(j + 1) * 128] = jnp.where(
                at_row, low[j:j + 1, :], 0.0
            ).astype(BF16)
        placed = dot(spread[...], pickt[...])
        return placed[:ROWS] + placed[ROWS:]

    few = lax.broadcasted_iota(jnp.int32, (CH, 128), 0)

    def same_cell(values):
        high, low = halves(values)
        mine = [few == uhi16[j:j + 1, :] for j in range(CH)]
        spread_h = [jnp.where(mine[j], high[j:j + 1, :], 0.0) for j in range(CH)]
        spread_l = [jnp.where(mine[j], low[j:j + 1, :], 0.0) for j in range(CH)]
        both = jnp.concatenate(
            [jnp.concatenate(spread_h, axis=1), jnp.concatenate(spread_l, axis=1)], axis=0
        ).astype(BF16)
        table = dot(both, uone[...])
        table = table[:CH] + table[CH:]
        uhi, ulo = uhi16[...], ulo16[...]
        out = jnp.zeros((CH, 128), F32)
        for r in range(CH):
            row = jnp.broadcast_to(table[r:r + 1, :], (CH, 128))
            found = jnp.take_along_axis(row, ulo, axis=1, mode="promise_in_bounds")
            out = jnp.where(uhi == r, found, out)
        return out

    def stage(values):
        for k in range(NB):
            fx[k] = values[4 * k:4 * k + 4, :]

    def send(parity):
        for m in FAR_FIRST:
            there = peer(m)
            sbuf[m - 1] = fx[kid[there]]
            pltpu.make_async_remote_copy(
                sbuf.at[m - 1], landing[parity].at[m], ssem, rsem.at[parity],
                device_id=(there,), device_id_type=MESH,
            ).start()

    def receive(parity):
        whole = pltpu.make_async_remote_copy(
            sbuf, landing[parity].at[pl.ds(1, NDEV - 1)], ssem, rsem.at[parity],
            device_id=(peer(1),), device_id_type=MESH,
        )
        whole.wait_recv()
        for k in range(NB):
            gx[4 * k:4 * k + 4, :] = landing[parity][at[k]]
        if parity < 2:
            whole.wait_send()

    def wait_all(sent, arrived, size, count, send_sem, recv_sem):
        pltpu.make_async_remote_copy(
            sent.at[pl.ds(size, size * count)], arrived.at[pl.ds(size, size * count)],
            send_sem, recv_sem, device_id=(peer(1),), device_id_type=MESH,
        ).wait()

    def patch(v):
        right = wr[...] * (v - pltpu.roll(v, COLS - 1, 1))
        down = wd[...] * (v - pltpu.roll(v, ROWS - 1, 0))
        return right - pltpu.roll(right, 1, 1) + down - pltpu.roll(down, 1, 0)

    def unfold(ref, c):
        return ref[pl.ds(c, ROWS, stride=4), :]

    def grid(ref):
        return jnp.concatenate([unfold(ref, c) for c in range(4)], axis=1)

    loads[2].wait()
    h = grid(depth)
    take(h, xg)

    place = [[], [], []]
    for axis in range(3):
        for j in range(HIGHN):
            for k in range(READS):
                b = reads[k, peer(high_mask(axis, j))]
                owner = lax.div(b, OWN)
                index = differ(low_index(axis, owner), low_index(axis, me), 3)
                place[axis].append(index * OWN + lax.rem(b, OWN))
    pl.semaphore_wait(barrier, NDEV - 1)

    for c in range(PIECES):
        for m in range(1, LOW):
            pltpu.make_async_remote_copy(
                ph1[c].at[pl.ds(0, OWN)], ph1[c].at[pl.ds(m * OWN, OWN)],
                s1.at[c], r1.at[c], device_id=(peer(low_mask(ROLES[c], m)),),
                device_id_type=MESH,
            ).start()
    last_col = lax.broadcasted_iota(jnp.int32, (ROWS, COLS), 1) == COLS - 1
    last_row = lax.broadcasted_iota(jnp.int32, (ROWS, COLS), 0) == ROWS - 1
    wr[...] = jnp.where(last_col, 0.0, 0.5 * (h + pltpu.roll(h, COLS - 1, 1)))
    wd[...] = jnp.where(last_row, 0.0, 0.5 * (h + pltpu.roll(h, ROWS - 1, 0)))
    loads[3].wait()
    mask = grid(wet).astype(F32)
    kw[...] = KAPPA * mask
    take(mask, kwj)
    kwj[...] = KAPPA * kwj[...]
    for c in range(PIECES):
        wait_all(ph1[c], ph1[c], OWN, LOW - 1, s1.at[c], r1.at[c])
        for j in range(HIGHN):
            part = pl.ds(j * READS, READS)
            goal = sb2 if j else rb2
            for k in range(READS):
                goal[c, j * READS + k] = ph1[c][place[ROLES[c]][j * READS + k]]
            if j:
                pltpu.make_async_remote_copy(
                    sb2.at[c, part], rb2.at[c, part], s2.at[c], r2.at[c],
                    device_id=(peer(high_mask(ROLES[c], j)),), device_id_type=MESH,
                ).start()

    stage(xg[...])
    send(2)

    for load in loads[4:]:
        load.wait()
    wgt[...] = kw[...] * grid(obs)
    take(wgt[...], obj)

    mins[...] = jnp.full((CH * 8, 128), 4096.0, F32)

    def earliest(i, carry):
        mine = row16[pl.ds(i, 1), :] * COLS + col16[pl.ds(i, 1), :]
        column = jnp.transpose(jnp.broadcast_to(mine.astype(F32), (128, 128)))
        number = (up + i * 128).astype(F32)
        for j in range(CH):
            other = (row16[j:j + 1, :] * COLS + col16[j:j + 1, :]).astype(F32)
            found = jnp.where(column == other, number, 4096.0)
            found = jnp.min(found.reshape(16, 8, 128), axis=0)
            mins[8 * j:8 * j + 8, :] = jnp.minimum(mins[8 * j:8 * j + 8, :], found)
        return carry

    lax.fori_loop(0, CH, earliest, 0)
    for j in range(CH):
        u = jnp.min(mins[8 * j:8 * j + 8, :], axis=0, keepdims=True).astype(jnp.int32)
        uhi16[j:j + 1, :] = lax.div(u, 128)
        ulo16[j:j + 1, :] = lax.rem(u, 128)
    for j in range(CH):
        ulo = ulo16[j:j + 1, :]
        column = jnp.transpose(jnp.broadcast_to(ulo.astype(F32), (128, 128)))
        uone[j * 128:(j + 1) * 128, :] = jnp.where(
            column == across.astype(F32), 1.0, 0.0
        ).astype(BF16)
        column = jnp.transpose(
            jnp.broadcast_to(col16[j:j + 1, :].astype(F32), (128, 128))
        )
        for c in range(4):
            pickt[j * 128:(j + 1) * 128, c * 128:(c + 1) * 128] = jnp.where(
                column == (across + c * 128).astype(F32), 1.0, 0.0
            ).astype(BF16)

    pltpu.make_async_remote_copy(
        sbuf, rbuf2.at[pl.ds(1, NDEV - 1)], ssem, rsem.at[2],
        device_id=(peer(1),), device_id_type=MESH,
    ).wait_send()
    for r in range(READS):
        for p in range(2):
            at_row = (2 * r + p) * CH
            uall[at_row:at_row + CH, :] = brows[0, r, pl.ds(p, CH, stride=2), :]
    for c in range(PIECES):
        wait_all(sb2.at[c], rb2.at[c], READS, HIGHN - 1, s2.at[c], r2.at[c])

    lane16 = lax.broadcasted_iota(jnp.int32, (CH, 128), 1)
    zero = jnp.zeros((2 * CH, 128), F32)
    diagonal = []
    for k in range(READS):
        owner = lax.div(reads[k, me], OWN)
        row = [differ(high_index(x, owner), high_index(x, me), 4) for x in range(3)]
        block = jnp.concatenate(
            [rb2[c, row[ROLES[c]] * READS + k] for c in range(PIECES)], axis=0
        )
        turned = pltpu.roll(block, 64, 1)
        if k % 2:
            both = [jnp.where(lane16 < 64, 0.0, v) for v in (turned, block)]
        else:
            both = [jnp.where(lane16 < 64, v, 0.0) for v in (block, turned)]
        both = jnp.concatenate(both, axis=0)
        diagonal.append(jnp.concatenate([zero, both] if k > 1 else [both, zero], axis=1))
    uy = bcols[0].reshape(READS * 64, COLS)
    inner = dot(jnp.concatenate(diagonal, axis=0), uy, HIGH)
    bathy = dot(jnp.transpose(uall[...]), inner, HIGH)
    src[...] = kw[...] * grid(sens) * bathy

    bgr[...] = src[...]
    take(src[...], pg)
    gx[...] = jnp.zeros((CH, 128), F32)

    def step(n, parity):
        stage(pg[...])
        send(parity)
        if parity == 0:
            @pl.when(n == 0)
            def _():
                receive(2)
                ew[...] = 0.5 * (xg[...] + gx[...])
                dia[...] = put(ew[...])
                gx[...] = jnp.zeros((CH, 128), F32)

        k = kw[...]
        e = bgr[...] + k * put(gx[...])
        turn = n == TURN
        s = jnp.where(turn, wgt[...] * e, src[...])
        seen[...] = jnp.where(turn, e, seen[...])
        e = jnp.where(turn, s, e)
        src[...] = s
        new = e - k * (patch(e) + dia[...] * e) + s
        bgr[...] = new
        ahead = n == TURN - 1
        take(jnp.where(ahead, wgt[...] * new, new), pg)
        receive(parity)
        x = ew[...] * gx[...]
        gx[...] = x
        scale = jnp.where(ahead, obj[...] * kwj[...], kwj[...])
        pg[...] = pg[...] + scale * same_cell(x)

    def pair(i, carry):
        step(2 * i, 0)
        step(2 * i + 1, 1)
        return carry

    seen[...] = src[...]
    lax.fori_loop(0, TURN, pair, 0)
    last = bgr[...] + kw[...] * put(gx[...])
    seen_obs = grid(obs) * seen[...]
    for c in range(4):
        wobs[pl.ds(c, ROWS, stride=4), :] = seen_obs[:, c * 128:(c + 1) * 128]
    store = pltpu.make_async_copy(wobs, wobs_hbm, outsem)
    store.start()

    grad = grid(sens) * last
    side = dot(uall[...], grad, HIGH)
    full = lax.dot_general(
        side, bcols[0].reshape(READS * 64, COLS), (((1,), (1,)), ((), ())),
        precision=HIGH, preferred_element_type=F32,
    )
    for r in range(READS):
        half = full[:, (r // 2) * 128:(r // 2 + 1) * 128]
        even = half[2 * r * CH:(2 * r + 1) * CH]
        odd = half[(2 * r + 1) * CH:(2 * r + 2) * CH]
        if r % 2:
            even = pltpu.roll(even, 64, 1)
        else:
            odd = pltpu.roll(odd, 64, 1)
        block = jnp.where(lane16 < 64, even, odd)
        for c in range(PIECES):
            gr[c, r] = block[c * PR:(c + 1) * PR]

    for c in range(PIECES):
        for j in range(1, HIGHN):
            pltpu.make_async_remote_copy(
                gr.at[c, pl.ds(0, READS)], gr.at[c, pl.ds(j * READS, READS)],
                s3.at[c], r3.at[c],
                device_id=(peer(high_mask(ROLES[c], j)),), device_id_type=MESH,
            ).start()
    lane = lax.broadcasted_iota(jnp.int32, (1, 128), 1)
    gather = []
    for axis in range(3):
        wt[...] = jnp.zeros((128, 128), F32)
        for j in range(HIGHN):
            for k in range(READS):
                s = j * READS + k
                owner = lax.div(reads[k, peer(high_mask(axis, j))], OWN)
                mine = high_index(axis, owner) == high_index(axis, me)
                index = jnp.where(mine, place[axis][s], -1)
                wt[s:s + 1, :] = jnp.where(lane == index, 1.0, 0.0)
        turned = jnp.transpose(wt[...])[:64, :64]
        gather.append(jnp.concatenate([turned, turned], axis=1).astype(BF16))
    for c in range(PIECES):
        wait_all(gr.at[c], gr.at[c], READS, HIGHN - 1, s3.at[c], r3.at[c])
        wide = jnp.concatenate([gr[c, :, i, :] for i in range(PR)], axis=1)
        wide = dot(gather[ROLES[c]], jnp.concatenate(halves(wide), axis=0).astype(BF16))
        for i in range(PR):
            sp[c, :, i, :] = wide[:, i * 128:(i + 1) * 128]
        for m in range(1, LOW):
            part = pl.ds(m * OWN, OWN)
            pltpu.make_async_remote_copy(
                sp.at[c, part], rp.at[c, part], s4.at[c], r4.at[c],
                device_id=(peer(low_mask(ROLES[c], m)),), device_id_type=MESH,
            ).start()
    for c in range(PIECES):
        wait_all(sp.at[c], rp.at[c], OWN, LOW - 1, s4.at[c], r4.at[c])
        total = sp[c, 0:OWN]
        for m in range(1, LOW):
            total = total + rp[c, m * OWN:(m + 1) * OWN]
        acc[c] = total
        for i in range(PR):
            at_lane = (c * PR + i) * 128
            hess[:, at_lane:at_lane + 128] = acc[c, :, i, :]
    store.wait()


def on_device(
    control, reads, neighbours, halo_cells, wet_mask, depth, sensitivity, obs_weight,
    basis_rows, basis_cols,
):
    flat = (ROWS * COLS // 128, 128)
    field = pltpu.VMEM((ROWS, COLS), F32)
    few = pltpu.VMEM((CH, 128), F32)
    few_int = pltpu.VMEM((CH, 128), jnp.int32)
    edges = CH * 128
    blocks = pltpu.VMEM((PIECES, LOW * OWN, PR, 128), F32)
    dma = pltpu.SemaphoreType.DMA
    vmem = pl.BlockSpec(memory_space=pltpu.VMEM)
    hess, wobs = pl.pallas_call(
        kernel,
        name="hessian_product",
        out_shape=(
            jax.ShapeDtypeStruct(control.shape, F32),
            jax.ShapeDtypeStruct(flat, F32),
        ),
        in_specs=[pl.BlockSpec(memory_space=pltpu.SMEM)] * 2
        + [pl.BlockSpec(memory_space=pltpu.HBM)] * 8,
        out_specs=(vmem, pl.BlockSpec(memory_space=pltpu.HBM)),
        scratch_shapes=[
            pltpu.VMEM(flat, F32),
            dma,
            pltpu.VMEM(control.shape, F32),
            pltpu.VMEM(halo_cells.shape, jnp.int32),
            pltpu.VMEM(flat, jnp.int32),
            pltpu.VMEM(flat, F32),
            pltpu.VMEM(flat, F32),
            pltpu.VMEM(flat, F32),
            pltpu.VMEM(basis_rows.shape, F32),
            pltpu.VMEM(basis_cols.shape, F32),
            dma((8,)),
            field, field, field, field, field, field, field,
            few,
            field,
            pltpu.VMEM((COLS, edges), BF16),
            pltpu.VMEM((edges, COLS), BF16),
            pltpu.VMEM((2 * ROWS, edges), BF16),
            pltpu.VMEM((edges, 128), BF16),
            few_int, few_int, few_int, few_int,
            pltpu.VMEM((CH * 8, 128), F32),
            few, few, few, few,
            pltpu.VMEM((NB, 4, 128), F32),
            few,
            pltpu.VMEM((NDEV - 1, 4, 128), F32),
            pltpu.VMEM((NDEV, 4, 128), F32),
            pltpu.VMEM((NDEV, 4, 128), F32),
            pltpu.VMEM((NDEV, 4, 128), F32),
            *[pltpu.VMEM((LOW * OWN, PR, 128), F32) for _ in range(PIECES)],
            blocks, blocks, blocks, blocks, blocks,
            pltpu.VMEM((128, 128), F32),
            pltpu.VMEM((128, 128), F32),
            pltpu.VMEM((PIECES, OWN, PR, 128), F32),
            pltpu.SMEM((NDEV,), jnp.int32),
            dma, dma((3,)),
            *[dma((PIECES,)) for _ in range(8)],
        ],
        compiler_params=pltpu.CompilerParams(
            collective_id=0, has_side_effects=True, vmem_limit_bytes=63 << 20
        ),
    )(
        reads.T, neighbours.T, control, halo_cells, wet_mask.reshape(flat), depth.reshape(flat),
        sensitivity.reshape(flat), obs_weight.reshape(flat), basis_rows, basis_cols,
    )
    return hess, wobs.reshape(-1)


def solution(mesh):
    return jax.shard_map(
        on_device,
        mesh=mesh,
        in_specs=(
            P("dom", None), P(), P(), P("dom", None, None), P("dom"), P("dom"), P("dom"),
            P("dom"), P("dom", None, None, None), P("dom", None, None, None),
        ),
        out_specs=(P("dom", None), P("dom")),
        check_vma=False,
    )
```
